256 devices in a mesh: dp: 16 (over x, y), seq: 16 (over z, core).
Axes of the slice: x: 4, y: 4, z: 8, core: 2. Of those that a mesh axis runs over, the one named last changes fastest.
Arguments:
- queries: bfloat16 [256, 128, 4096], P(('dp', 'seq')), parts along dimension 0, may hold values from -6 to 6
- outputs: bfloat16 [256, 128, 4096], P(('dp', 'seq')), parts along dimension 0, may hold values from -3 to 3
- out_grads: bfloat16 [256, 128, 4096], P(('dp', 'seq')), parts along dimension 0, may hold values from -12 to 12
- resp_keys: bfloat16 [256, 128, 512], P(('dp', 'seq')), parts along dimension 0, may hold values from -6 to 6
- resp_values: bfloat16 [256, 128, 512], P(('dp', 'seq')), parts along dimension 0, may hold values from -6 to 6
- lengths: int32 [256], P('dp'), parts along dimension 0, may hold values from 1 to 128, 1024 in all
- prompt_keys: bfloat16 [12288, 512], P(('dp', 'seq')), parts along dimension 0, may hold values from -6 to 6
- prompt_values: bfloat16 [12288, 512], P(('dp', 'seq')), parts along dimension 0, may hold values from -6 to 6
Outputs:
- query_grads: bfloat16 [256, 128, 4096], P(('dp', 'seq')), parts along dimension 0
- resp_key_grads: bfloat16 [256, 128, 512], P(('dp', 'seq')), parts along dimension 0
- resp_value_grads: bfloat16 [256, 128, 512], P(('dp', 'seq')), parts along dimension 0
- prompt_key_grads: bfloat16 [12288, 512], P(('dp', 'seq')), parts along dimension 0
- prompt_value_grads: bfloat16 [12288, 512], P(('dp', 'seq')), parts along dimension 0
The draws below stay inside these ranges and needn't reach their ends.
There are 16 independent parts, one for each index of `dp`. The reference program is written for one: setup_inputs(seed, part) draws one part's arguments, and reference() takes and returns one part's arrays. A program takes and returns all parts, laid end to end along the dimension named above; each array names one. Nothing has to cross between parts.
All inputs are finite; a program needn't handle non-finite values.
Results may differ from the reference program's by a relative error of at most 0.0055.
Values may be sent and summed in bfloat16 or wider, within the bound.
A program may use at most 64 MiB of HBM per device.

```python
import math
import jax
import jax.numpy as jnp
import numpy as np
from jax import lax

HEADS = 32
KV_HEADS = 4
HEAD_DIM = 128
RESP_LEN = 128
PROMPT = 768
RESPONSES = 16


def draw_queries(key, part):
    key = jax.random.fold_in(key, 3)
    drawn = jnp.clip(jax.random.normal(key, (RESPONSES, RESP_LEN, HEADS, HEAD_DIM), jnp.float32), -4.0, 4.0)
    return drawn.reshape(RESPONSES, RESP_LEN, HEADS * HEAD_DIM).astype(jnp.bfloat16)


def draw_prompt_keys(key, part):
    key = jax.random.fold_in(key, 5)
    drawn = jnp.clip(jax.random.normal(key, (PROMPT, KV_HEADS * HEAD_DIM), jnp.float32), -4.0, 4.0)
    return drawn.astype(jnp.bfloat16)


def block_scale(rng, dims, shards, least, high):
    level, own = 1.0, jax.random.fold_in(rng, 6)
    for dim, shards_of in shards:
        draws = jnp.exp(jax.random.uniform(jax.random.fold_in(own, dim), (shards_of,), jnp.float32, least / len(shards), high / len(shards)))
        level = level * jnp.repeat(draws, dims[dim] // shards_of).reshape([-1 if axis == dim else 1 for axis in range(len(dims))])
    return level


def profile(number_of, total, limit, slope):
    portions = [(1 << 20) // math.isqrt(standing ** slope) + 1 for standing in range(2, number_of + 1)]
    surplus, counts = total - limit - (number_of - 1), [1] * (number_of - 1)
    while surplus > 0:
        movable = [i for i in range(number_of - 1) if counts[i] < limit]
        pool, left = sum([portions[i] for i in movable]), surplus
        for i in movable:
            extra = min(limit - counts[i], max(1, left * portions[i] // pool), surplus)
            counts[i] = counts[i] + extra
            surplus = surplus - extra
    return np.array([limit] + counts)


def ragged_sizes(rng, amount, total, limit, skew):
    if amount == 2:
        one = jax.random.randint(rng, (), max(1, total - limit), min(limit, total - 1) + 1)
        return jnp.stack([one, total - one])
    sizes = jnp.asarray(profile(amount, total, limit, skew), jnp.int32)
    pairs = (amount - 1) // 2
    giver, taker = sizes[1:1 + 2 * pairs:2], sizes[2:2 + 2 * pairs:2]
    room = jnp.minimum(giver - 1, limit - taker)
    moved = jax.random.randint(jax.random.fold_in(rng, 1), (pairs,), 0, 1 << 20) % (room + 1)
    sizes = sizes.at[1:1 + 2 * pairs:2].set(giver - moved).at[2:2 + 2 * pairs:2].set(taker + moved)
    return sizes[jax.random.permutation(jax.random.fold_in(rng, 2), amount)]


def centred(stream_key, dims, deviation, limit, cuts=(), held_as=jnp.bfloat16):
    loudness = block_scale(stream_key, dims, cuts, -0.22, 0.18) if cuts else 1.0
    values = jax.random.normal(stream_key, dims, jnp.float32) * deviation * loudness
    return jnp.minimum(jnp.maximum(values, -limit), limit).astype(held_as)


def setup_inputs(seed: int = 0, part: int = 0) -> dict:
    key_of = jax.random.split(jax.random.key(seed), 9)
    part_splits = jax.random.split(jax.random.fold_in(key_of[8], part), 9)
    return {
        "queries": draw_queries(jax.random.fold_in(jax.random.fold_in(key_of[8], part), 71), part),
        "outputs": centred(part_splits[1], (RESPONSES, RESP_LEN, HEADS * HEAD_DIM), 0.5, 3.0, ((0, 16),)),
        "out_grads": centred(part_splits[2], (RESPONSES, RESP_LEN, HEADS * HEAD_DIM), 2.0, 12.0, ((0, 16),)),
        "resp_keys": centred(part_splits[3], (RESPONSES, RESP_LEN, KV_HEADS * HEAD_DIM), 1.0, 6.0, ((0, 16),)),
        "resp_values": centred(part_splits[4], (RESPONSES, RESP_LEN, KV_HEADS * HEAD_DIM), 1.0, 6.0, ((0, 16),)),
        "lengths": ragged_sizes(part_splits[5], RESPONSES, RESPONSES * RESP_LEN // 2, RESP_LEN, 2).astype(jnp.int32),
        "prompt_keys": draw_prompt_keys(jax.random.fold_in(jax.random.fold_in(key_of[8], part), 71), part),
        "prompt_values": centred(part_splits[7], (PROMPT, KV_HEADS * HEAD_DIM), 1.0, 6.0, ((0, 16),)),
    }


def group_grads(query_rows, output_rows, grad_rows, key_block, value_block, length):
    softmax_scale = HEAD_DIM ** -0.5
    position = lax.iota(jnp.int32, RESP_LEN)
    key_position = lax.iota(jnp.int32, PROMPT + RESP_LEN)
    visible = (key_position[None, :] < PROMPT) | (key_position[None, :] - PROMPT <= position[:, None])
    live_rows = position < length
    scores = jnp.einsum("tgd,jd->gtj", query_rows.astype(jnp.float32), key_block.astype(jnp.float32)) * softmax_scale
    top_score = jnp.max(jnp.where(visible[None], scores, -1e30), axis=2)
    exp_total = jnp.sum(jnp.where(visible[None], jnp.exp(scores - top_score[:, :, None]), 0.0), axis=2)
    log_total = top_score + jnp.log(exp_total)
    usable = (visible & live_rows[:, None])[None]
    probability = jnp.where(usable, jnp.exp(scores - log_total[:, :, None]), 0.0)
    row_delta = jnp.sum(grad_rows.astype(jnp.float32) * output_rows.astype(jnp.float32), axis=2).T
    prob_grad = jnp.einsum("tgd,jd->gtj", grad_rows.astype(jnp.float32), value_block.astype(jnp.float32))
    score_grad = (probability * (prob_grad - row_delta[:, :, None])).astype(jnp.bfloat16)
    weights = probability.astype(jnp.bfloat16)
    value_grad = jnp.einsum("gtj,tgd->jd", weights.astype(jnp.float32), grad_rows.astype(jnp.float32))
    key_grad = jnp.einsum("gtj,tgd->jd", score_grad.astype(jnp.float32), query_rows.astype(jnp.float32)) * softmax_scale
    query_grad = jnp.einsum("gtj,jd->tgd", score_grad.astype(jnp.float32), key_block.astype(jnp.float32)) * softmax_scale
    return query_grad, key_grad, value_grad


def one_response(query_all, output_all, grad_all, resp_key_rows, resp_value_rows, length, prompt_keys, prompt_values):
    per_group = HEADS // KV_HEADS
    width = per_group * HEAD_DIM
    query_parts = []
    resp_key_parts = []
    resp_value_parts = []
    prompt_key_parts = []
    prompt_value_parts = []
    for group_index in range(KV_HEADS):
        low = group_index * width
        query_rows = query_all[:, low:low + width].reshape(RESP_LEN, per_group, HEAD_DIM)
        output_rows = output_all[:, low:low + width].reshape(RESP_LEN, per_group, HEAD_DIM)
        grad_rows = grad_all[:, low:low + width].reshape(RESP_LEN, per_group, HEAD_DIM)
        column = group_index * HEAD_DIM
        key_block = jnp.concatenate([prompt_keys[:, column:column + HEAD_DIM], resp_key_rows[:, column:column + HEAD_DIM]], axis=0)
        value_block = jnp.concatenate([prompt_values[:, column:column + HEAD_DIM], resp_value_rows[:, column:column + HEAD_DIM]], axis=0)
        query_grad, key_grad, value_grad = group_grads(query_rows, output_rows, grad_rows, key_block, value_block, length)
        query_parts.append(query_grad.reshape(RESP_LEN, width))
        prompt_key_parts.append(key_grad[:PROMPT])
        resp_key_parts.append(key_grad[PROMPT:])
        prompt_value_parts.append(value_grad[:PROMPT])
        resp_value_parts.append(value_grad[PROMPT:])
    return (jnp.concatenate(query_parts, axis=1).astype(jnp.bfloat16),
            jnp.concatenate(resp_key_parts, axis=1).astype(jnp.bfloat16),
            jnp.concatenate(resp_value_parts, axis=1).astype(jnp.bfloat16),
            jnp.concatenate(prompt_key_parts, axis=1),
            jnp.concatenate(prompt_value_parts, axis=1))


def reference(queries, outputs, out_grads, resp_keys, resp_values, lengths, prompt_keys, prompt_values):
    def accumulate(running, response):
        query_all, output_all, grad_all, key_rows, value_rows, length = response
        query_grad, key_grad, value_grad, prompt_key_part, prompt_value_part = one_response(
            query_all, output_all, grad_all, key_rows, value_rows, length, prompt_keys, prompt_values)
        return (running[0] + prompt_key_part, running[1] + prompt_value_part), (query_grad, key_grad, value_grad)

    zero_sum = jnp.zeros((PROMPT, KV_HEADS * HEAD_DIM), jnp.float32)
    (key_sum, value_sum), (query_grads, resp_key_grads, resp_value_grads) = lax.scan(
        accumulate, (zero_sum, zero_sum), (queries, outputs, out_grads, resp_keys, resp_values, lengths))
    return query_grads, resp_key_grads, resp_value_grads, key_sum.astype(jnp.bfloat16), value_sum.astype(jnp.bfloat16)
```

```python
import jax
import jax.numpy as jnp
from jax import lax
from jax.experimental import pallas as pl
from jax.experimental.pallas import tpu as pltpu
from jax.sharding import PartitionSpec as P

F32 = jnp.float32
BF16 = jnp.bfloat16
HEAD = 128
ROWS = 128
GROUPS = 4
PAIRS = 4
CHIPS = 8
OWN = 48
PROMPT = 2 * CHIPS * OWN
KEYS = PROMPT + ROWS
SCALE = HEAD**-0.5
SCALE2 = SCALE * 1.4426950408889634
BLOCK = 64


def dot(a, b):
    return jnp.dot(a, b, preferred_element_type=F32)


def dot_nt(a, b):
    return lax.dot_general(a, b, (((1,), (1,)), ((), ())), preferred_element_type=F32)


def kernel(
    q_hbm, o_hbm, g_hbm, rk_hbm, rv_hbm, len_ref, pk_hbm, pv_hbm,
    dq_hbm, drk_hbm, drv_hbm, dpk_hbm, dpv_hbm,
    q, o, g, rk, rv, kv, s_scr, dp_scr, p_scr, ds_scr, delta, acc, cp,
    sib_out, sib_in, st1_out, st1_in, st2_out, st2_in, dq, drk, drv, dpk, dpv,
    in_sem, own_sem, out_sem, gs_sem, gr_sem, ss_sem, sr_sem,
):
    me = lax.axis_index("seq")
    z = me // 2
    c = lax.rem(me, 2)
    sign = 1 - 2 * c
    sibling = me + sign

    def chip(k):
        return lax.rem(z + k + 16, CHIPS)

    def device(k):
        return chip(k) * 2 + c

    loads = []
    for i, (src, dst) in enumerate(((g_hbm, g), (o_hbm, o), (q_hbm, q), (rk_hbm, rk), (rv_hbm, rv))):
        loads.append(pltpu.make_async_copy(src.at[0], dst, in_sem.at[i]))
    own = kv.at[:, c, z]
    for h in range(GROUPS):
        cols = pl.ds(h * HEAD, HEAD)
        pltpu.make_async_copy(pk_hbm.at[:, cols], kv.at[h, c, z, :, pl.ds(0, HEAD)], own_sem).start()
        pltpu.make_async_copy(pv_hbm.at[:, cols], kv.at[h, c, z, :, pl.ds(HEAD, HEAD)], own_sem).start()
    for load in loads:
        load.start()

    barrier = pltpu.get_barrier_semaphore()
    for target in (device(1), device(-1), device(2), device(-2), sibling):
        pl.semaphore_signal(barrier, inc=1, device_id={"seq": target}, device_id_type=pl.DeviceIdType.MESH)
    pl.semaphore_wait(barrier, 5)
    pltpu.make_async_copy(own, own, own_sem).wait()

    def remote(src, dst, send, recv, target):
        return pltpu.make_async_remote_copy(
            src_ref=src, dst_ref=dst, send_sem=send, recv_sem=recv,
            device_id={"seq": target}, device_id_type=pl.DeviceIdType.MESH,
        )

    def gather(h, slot, origin, target):
        block = kv.at[h, c, chip(origin)]
        return remote(block, block, gs_sem.at[h, slot], gr_sem.at[h, slot], device(target))

    def gather_in(h, slot, origin):
        block = kv.at[h, c, chip(origin)]
        return remote(block, block, gs_sem.at[h, slot], gr_sem.at[h, slot], me)

    stage1 = ((0, 1), (1, -1), (2, 2), (3, -2))
    for h in range(GROUPS):
        for slot, step in stage1:
            gather(h, slot, 0, step).start()

    loads[0].wait()
    loads[1].wait()
    ones = jnp.ones((8, HEAD), BF16)

    def two(ref, pair):
        col = pl.multiple_of(pair * 2 * HEAD, 2 * HEAD)
        return jnp.concatenate([ref[:, pl.ds(col, HEAD)], ref[:, pl.ds(col + HEAD, HEAD)]], axis=0)

    def delta_pair(i, _):
        product = two(g, i).astype(F32) * two(o, i).astype(F32)
        high = product.astype(BF16)
        low = (product - high.astype(F32)).astype(BF16)
        delta[i] = dot_nt(ones, high) + dot_nt(ones, low)
        return 0

    lax.fori_loop(0, GROUPS * PAIRS, delta_pair, 0)
    for load in loads[2:]:
        load.wait()

    def forward(h, _):
        gather_in(h, 2, -2).wait_recv()
        gather(h, 4, -2, 1).start()
        gather_in(h, 3, 2).wait_recv()
        gather(h, 5, 2, -1).start()
        gather(h, 6, -2 * sign, 2 * sign).start()
        return 0

    lax.fori_loop(0, GROUPS, forward, 0)

    def half(h, core):
        return kv.at[h, core]

    def sib_gather(h, core):
        return remote(half(h, core), half(h, core), gs_sem.at[h, 7], gr_sem.at[h, 7], sibling)

    def pass_on(h):
        gather_in(h, 0, -1).wait_recv()
        gather_in(h, 1, 1).wait_recv()
        gather_in(h, 4, -3).wait_recv()
        gather_in(h, 5, 3).wait_recv()
        gather_in(h, 6, 4).wait_recv()
        sib_gather(h, c).start()

    def sib_scatter(h):
        return remote(sib_out.at[h], sib_in.at[h], ss_sem.at[h, 0], sr_sem.at[h, 0], sibling)

    def stage1_scatter(h, slot, target):
        return remote(st1_out.at[h, slot], st1_in.at[h, slot], ss_sem.at[h, 1 + slot], sr_sem.at[h, 1 + slot], target)

    def stage2_scatter(h, slot, target):
        return remote(st2_out.at[h, slot], st2_in.at[h, slot], ss_sem.at[h, 6 + slot], sr_sem.at[h, 6 + slot], target)

    first = ((0, 1, 3), (1, -1, -3), (2, 2 * sign, 4), (3, 1, 1), (4, -1, -1))

    def scatter_a(h):
        sib_out[h] = acc[1 - c].astype(BF16)
        sib_scatter(h).start()
        cp[h] = acc[c]

    def scatter_b(h):
        sib_scatter(h).wait_recv()
        cp[h] += sib_in[h].astype(F32)
        for slot, step, owner in first:
            st1_out[h, slot] = cp[h, chip(owner)].astype(BF16)
            stage1_scatter(h, slot, device(step)).start()

    def scatter_c(h):
        for slot in range(3):
            stage1_scatter(h, slot, me).wait_recv()
        cp[h, chip(2 * sign)] += st1_in[h, 2].astype(F32)
        st2_out[h, 0] = (cp[h, chip(2)] + st1_in[h, 0].astype(F32)).astype(BF16)
        stage2_scatter(h, 0, device(2)).start()
        st2_out[h, 1] = (cp[h, chip(-2)] + st1_in[h, 1].astype(F32)).astype(BF16)
        stage2_scatter(h, 1, device(-2)).start()

    def scatter_d(h):
        stage1_scatter(h, 3, me).wait_recv()
        stage1_scatter(h, 4, me).wait_recv()
        stage2_scatter(h, 0, me).wait_recv()
        stage2_scatter(h, 1, me).wait_recv()
        total = (
            cp[h, z] + st1_in[h, 3].astype(F32) + st1_in[h, 4].astype(F32)
            + st2_in[h, 0].astype(F32) + st2_in[h, 1].astype(F32)
        ).astype(BF16)
        col = pl.ds(pl.multiple_of(h * HEAD, HEAD), HEAD)
        dpk[:, col] = total[:, :HEAD]
        dpv[:, col] = total[:, HEAD:]

    token = lax.rem(lax.broadcasted_iota(jnp.int32, (1, 2 * ROWS), 1), ROWS)
    live = token < len_ref[me]
    causal = lax.broadcasted_iota(jnp.int32, (ROWS, 2 * ROWS), 0) <= lax.rem(
        lax.broadcasted_iota(jnp.int32, (ROWS, 2 * ROWS), 1), ROWS
    )

    def column(h):
        return pl.ds(pl.multiple_of(h * HEAD, HEAD), HEAD)

    def keys(h):
        return kv[h, :, :, :, pl.ds(0, HEAD)].reshape(PROMPT, HEAD)

    def values(h):
        return kv[h, :, :, :, pl.ds(HEAD, HEAD)].reshape(PROMPT, HEAD)

    def scores(h, p):
        b = p % 2
        q2 = two(q, h * PAIRS + p)
        g2 = two(g, h * PAIRS + p)
        s_scr[b, PROMPT:] = jnp.where(causal, dot_nt(rk[:, column(h)], q2), -1e30)
        s_scr[b, :PROMPT] = dot_nt(keys(h), q2)
        dp_scr[b, PROMPT:] = dot_nt(rv[:, column(h)], g2)
        dp_scr[b, :PROMPT] = dot_nt(values(h), g2)

    def softmax(h, p):
        b = p % 2
        top = jnp.full((8, 2 * ROWS), -1e30, F32)
        for r in range(0, KEYS, BLOCK):
            top = jnp.maximum(top, jnp.max(s_scr[b, r : r + BLOCK].reshape(BLOCK // 8, 8, 2 * ROWS), axis=0))
        top = jnp.max(top, axis=0, keepdims=True) * SCALE2
        total = jnp.zeros((8, 2 * ROWS), F32)
        for r in range(0, KEYS, BLOCK):
            e = jnp.exp2(s_scr[b, r : r + BLOCK] * SCALE2 - top)
            total = total + jnp.sum(e.reshape(BLOCK // 8, 8, 2 * ROWS), axis=0)
            s_scr[b, r : r + BLOCK] = e
        inverse = jnp.where(live, 1.0 / jnp.sum(total, axis=0, keepdims=True), 0.0)
        row_delta = delta[h * PAIRS + p][0:1]
        for r in range(0, KEYS, BLOCK):
            probability = s_scr[b, r : r + BLOCK] * inverse
            p_scr[p, r : r + BLOCK] = probability.astype(BF16)
            ds_scr[h * PAIRS + p, r : r + BLOCK] = (
                probability * (dp_scr[b, r : r + BLOCK] - row_delta)
            ).astype(BF16)

    pass_on(0)

    def group(h, _):
        sib_gather(h, 1 - c).wait_recv()
        scores(h, 0)
        for p in range(PAIRS):
            if p + 1 < PAIRS:
                scores(h, p + 1)
            softmax(h, p)
            if p == 1:
                @pl.when(h >= 1)
                def _():
                    scatter_b(h - 1)
            if p == 2:
                @pl.when(h < GROUPS - 1)
                def _():
                    pass_on(h + 1)
        g8 = jnp.concatenate([two(g, h * PAIRS + p) for p in range(PAIRS)], axis=0)
        q8 = jnp.concatenate([two(q, h * PAIRS + p) for p in range(PAIRS)], axis=0)
        dv = dot(jnp.concatenate([p_scr[p] for p in range(PAIRS)], axis=1), g8)
        dk = dot(jnp.concatenate([ds_scr[h * PAIRS + p] for p in range(PAIRS)], axis=1), q8) * SCALE
        acc[:, :, :, pl.ds(0, HEAD)] = dk[:PROMPT].reshape(2, CHIPS, OWN, HEAD)
        acc[:, :, :, pl.ds(HEAD, HEAD)] = dv[:PROMPT].reshape(2, CHIPS, OWN, HEAD)
        scatter_a(h)
        drk[:, column(h)] = dk[PROMPT:].astype(BF16)
        drv[:, column(h)] = dv[PROMPT:].astype(BF16)
        @pl.when(h >= 2)
        def _():
            scatter_c(h - 2)
        return 0

    lax.fori_loop(0, GROUPS, group, 0)

    out_rk = pltpu.make_async_copy(drk, drk_hbm.at[0], out_sem.at[0])
    out_rv = pltpu.make_async_copy(drv, drv_hbm.at[0], out_sem.at[1])
    out_rk.start()
    out_rv.start()

    def query_grads(h):
        kt = jnp.concatenate([keys(h), rk[:, column(h)]], axis=0).T
        for p in range(PAIRS):
            grad = dot(kt, ds_scr[h * PAIRS + p]) * SCALE
            col = pl.multiple_of((h * PAIRS + p) * 2 * HEAD, 2 * HEAD)
            dq[:, pl.ds(col, HEAD)] = grad[:, :ROWS].T.astype(BF16)
            dq[:, pl.ds(col + HEAD, HEAD)] = grad[:, ROWS:].T.astype(BF16)

    def dq_out(i):
        cols = pl.ds(i * 2048, 2048)
        return pltpu.make_async_copy(dq.at[:, cols], dq_hbm.at[0, :, cols], out_sem.at[2 + i])

    def query_loop(h, _):
        query_grads(h)
        return 0

    lax.fori_loop(0, 2, query_loop, 0)
    dq_out(0).start()
    scatter_b(3)
    scatter_c(2)
    lax.fori_loop(2, 4, query_loop, 0)
    dq_out(1).start()
    scatter_d(0)
    scatter_d(1)
    scatter_c(3)
    scatter_d(2)
    scatter_d(3)
    out_pk = pltpu.make_async_copy(dpk, dpk_hbm, out_sem.at[4])
    out_pv = pltpu.make_async_copy(dpv, dpv_hbm, out_sem.at[5])
    out_pk.start()
    out_pv.start()

    def drain(h, _):
        for slot, step in stage1:
            gather(h, slot, 0, step).wait_send()
        gather(h, 4, -2, 1).wait_send()
        gather(h, 5, 2, -1).wait_send()
        gather(h, 6, -2 * sign, 2 * sign).wait_send()
        sib_gather(h, c).wait_send()
        sib_scatter(h).wait_send()
        for slot, step, owner in first:
            stage1_scatter(h, slot, device(step)).wait_send()
        stage2_scatter(h, 0, device(2)).wait_send()
        stage2_scatter(h, 1, device(-2)).wait_send()
        return 0

    lax.fori_loop(0, GROUPS, drain, 0)
    for copy in (out_rk, out_rv, dq_out(0), dq_out(1), out_pk, out_pv):
        copy.wait()


def local(queries, outputs, out_grads, resp_keys, resp_values, lengths, prompt_keys, prompt_values):
    any_spec = pl.BlockSpec(memory_space=pl.ANY)
    wide = (ROWS, GROUPS * PAIRS * 2 * HEAD)
    narrow = (ROWS, GROUPS * HEAD)
    block = (OWN, 2 * HEAD)
    return pl.pallas_call(
        kernel,
        name="grads",
        out_shape=[
            jax.ShapeDtypeStruct((1,) + wide, BF16),
            jax.ShapeDtypeStruct((1,) + narrow, BF16),
            jax.ShapeDtypeStruct((1,) + narrow, BF16),
            jax.ShapeDtypeStruct((OWN, GROUPS * HEAD), BF16),
            jax.ShapeDtypeStruct((OWN, GROUPS * HEAD), BF16),
        ],
        in_specs=[any_spec] * 5 + [pl.BlockSpec(memory_space=pltpu.SMEM)] + [any_spec] * 2,
        out_specs=[any_spec] * 5,
        scratch_shapes=[
            pltpu.VMEM(wide, BF16),
            pltpu.VMEM(wide, BF16),
            pltpu.VMEM(wide, BF16),
            pltpu.VMEM(narrow, BF16),
            pltpu.VMEM(narrow, BF16),
            pltpu.VMEM((GROUPS, 2, CHIPS) + block, BF16),
            pltpu.VMEM((2, KEYS, 2 * ROWS), F32),
            pltpu.VMEM((2, KEYS, 2 * ROWS), F32),
            pltpu.VMEM((PAIRS, KEYS, 2 * ROWS), BF16),
            pltpu.VMEM((GROUPS * PAIRS, KEYS, 2 * ROWS), BF16),
            pltpu.VMEM((GROUPS * PAIRS, 8, 2 * ROWS), F32),
            pltpu.VMEM((2, CHIPS) + block, F32),
            pltpu.VMEM((GROUPS, CHIPS) + block, F32),
            pltpu.VMEM((GROUPS, CHIPS) + block, BF16),
            pltpu.VMEM((GROUPS, CHIPS) + block, BF16),
            pltpu.VMEM((GROUPS, 5) + block, BF16),
            pltpu.VMEM((GROUPS, 5) + block, BF16),
            pltpu.VMEM((GROUPS, 2) + block, BF16),
            pltpu.VMEM((GROUPS, 2) + block, BF16),
            pltpu.VMEM(wide, BF16),
            pltpu.VMEM(narrow, BF16),
            pltpu.VMEM(narrow, BF16),
            pltpu.VMEM((OWN, GROUPS * HEAD), BF16),
            pltpu.VMEM((OWN, GROUPS * HEAD), BF16),
            pltpu.SemaphoreType.DMA((5,)),
            pltpu.SemaphoreType.DMA,
            pltpu.SemaphoreType.DMA((6,)),
            pltpu.SemaphoreType.DMA((GROUPS, 8)),
            pltpu.SemaphoreType.DMA((GROUPS, 8)),
            pltpu.SemaphoreType.DMA((GROUPS, 8)),
            pltpu.SemaphoreType.DMA((GROUPS, 8)),
        ],
        compiler_params=pltpu.CompilerParams(
            collective_id=0, has_side_effects=True, vmem_limit_bytes=56 * 2**20
        ),
        cost_estimate=pl.CostEstimate(flops=4700000000, bytes_accessed=5000000, transcendentals=3670016),
    )(queries, outputs, out_grads, resp_keys, resp_values, lengths, prompt_keys, prompt_values)


def solution(mesh):
    rows = P(("dp", "seq"), None, None)
    prompt = P(("dp", "seq"), None)
    return jax.shard_map(
        local,
        mesh=mesh,
        in_specs=(rows, rows, rows, rows, rows, P("dp"), prompt, prompt),
        out_specs=(rows, rows, rows, prompt, prompt),
        check_vma=False,
    )
```

```python
import functools

import jax
import jax.numpy as jnp
from jax import lax
from jax.experimental import pallas as pl
from jax.experimental.pallas import tpu as pltpu
from jax.sharding import PartitionSpec as P

F32 = jnp.float32
BF16 = jnp.bfloat16
HEAD = 128
ROWS = 128
GROUPS = 4
PAIRS = 4
WIDE = 2 * ROWS
CHIPS = 8
OWN = 48
HALF = CHIPS * OWN
PROMPT = 2 * HALF
KEYS = PROMPT + ROWS
BLOCK = 256
SCALE = HEAD**-0.5
SCALE2 = SCALE * 1.4426950408889634
MESH = pl.DeviceIdType.MESH


def dot(a, b):
    return jnp.dot(a, b, preferred_element_type=F32)


def dot_nt(a, b):
    return lax.dot_general(a, b, (((1,), (1,)), ((), ())), preferred_element_type=F32)


def fold(x, op):
    return op(x.reshape(x.shape[0] // 8, 8, x.shape[1]), axis=0)


def weave(*lists):
    steps = max(len(entry) for entry in lists)
    done = [0] * len(lists)
    for step in range(steps):
        for i, entry in enumerate(lists):
            while done[i] < len(entry) and done[i] * steps < (step + 1) * len(entry):
                entry[done[i]]()
                done[i] += 1


def kernel(
    q_hbm, o_hbm, g_hbm, rk_hbm, rv_hbm, len_ref, pk_hbm, pv_hbm,
    dq_hbm, drk_hbm, drv_hbm, dpk_hbm, dpv_hbm,
    q, o, g, rk, rv, kv, s_scr, rs_scr, rdp_scr, p_scr, rp_scr, ds_scr, delta, acc, cp,
    sib_out, sib_in, st1_out, st1_in, st2_out, st2_in, dq, drk, drv, dpk, dpv,
    in_sem, own_sem, out_sem, gs_sem, gr_sem, ss_sem, sr_sem,
):
    me = lax.axis_index("seq")
    z = me // 2
    c = lax.rem(me, 2)
    sign = 1 - 2 * c
    sibling = me + sign

    def chip(k):
        return lax.rem(z + k + 16, CHIPS)

    def device(k):
        return chip(k) * 2 + c

    def rows_of(zz):
        return pl.ds(pl.multiple_of(zz * OWN, 16), OWN)

    def half_of(core):
        return pl.ds(pl.multiple_of(core * HALF, HALF), HALF)

    def block_of(zz):
        return pl.ds(pl.multiple_of((c * CHIPS + zz) * OWN, 16), OWN)

    loads = []
    for i, (src, dst) in enumerate(((g_hbm, g), (o_hbm, o), (q_hbm, q), (rk_hbm, rk), (rv_hbm, rv))):
        loads.append(pltpu.make_async_copy(src.at[0], dst, in_sem.at[i]))
    own = kv.at[:, block_of(z)]
    for h in range(GROUPS):
        cols = pl.ds(h * HEAD, HEAD)
        pltpu.make_async_copy(pk_hbm.at[:, cols], kv.at[h, block_of(z), pl.ds(0, HEAD)], own_sem).start()
        pltpu.make_async_copy(pv_hbm.at[:, cols], kv.at[h, block_of(z), pl.ds(HEAD, HEAD)], own_sem).start()
    for load in loads:
        load.start()

    barrier = pltpu.get_barrier_semaphore()
    for target in (device(1), device(-1), device(2), device(-2), sibling):
        pl.semaphore_signal(barrier, inc=1, device_id={"seq": target}, device_id_type=MESH)
    pl.semaphore_wait(barrier, 5)
    pltpu.make_async_copy(own, own, own_sem).wait()

    def remote(src, dst, send, recv, target):
        return pltpu.make_async_remote_copy(
            src_ref=src, dst_ref=dst, send_sem=send, recv_sem=recv,
            device_id={"seq": target}, device_id_type=MESH,
        )

    def gather(h, slot, origin, target):
        block = kv.at[h, block_of(chip(origin))]
        return remote(block, block, gs_sem.at[h, slot], gr_sem.at[h, slot], device(target))

    def gather_wait(h, slot, origin):
        gather(h, slot, origin, 1).wait_recv()

    near = ((0, 1), (1, -1), (2, 2), (3, -2))

    def gather_near(h):
        for slot, step in near:
            gather(h, slot, 0, step).start()

    def gather_far(h):
        gather_wait(h, 2, -2)
        gather(h, 4, -2, 1).start()
        gather_wait(h, 3, 2)
        gather(h, 5, 2, -1).start()
        gather(h, 6, -2 * sign, 2 * sign).start()

    def sib_gather(h, core):
        part = kv.at[h, half_of(core)]
        return remote(part, part, gs_sem.at[h, 7], gr_sem.at[h, 7], sibling)

    def pass_on(h):
        for slot, origin in ((0, -1), (1, 1), (4, -3), (5, 3), (6, 4)):
            gather_wait(h, slot, origin)
        sib_gather(h, c).start()

    def sib_scatter(h):
        return remote(sib_out.at[h], sib_in.at[h], ss_sem.at[h, 0], sr_sem.at[h, 0], sibling)

    def scatter1(h, slot, step):
        return remote(
            st1_out.at[h, slot], st1_in.at[h, slot], ss_sem.at[h, 1 + slot], sr_sem.at[h, 1 + slot], device(step)
        )

    def scatter2(h, slot, step):
        return remote(
            st2_out.at[h, slot], st2_in.at[h, slot], ss_sem.at[h, 6 + slot], sr_sem.at[h, 6 + slot], device(step)
        )

    first = ((0, 1, 3), (1, -1, -3), (2, 2 * sign, 4), (3, 1, 1), (4, -1, -1))

    def scatter_a(h):
        sib_out[h] = acc[half_of(1 - c)].astype(BF16)
        sib_scatter(h).start()
        cp[h] = acc[half_of(c)]

    def scatter_b(h):
        sib_scatter(h).wait_recv()
        cp[h] += sib_in[h].astype(F32)
        for slot, step, owner in first:
            st1_out[h, slot] = cp[h, rows_of(chip(owner))].astype(BF16)
            scatter1(h, slot, step).start()

    def scatter_c(h):
        for slot in range(3):
            scatter1(h, slot, 1).wait_recv()
        cp[h, rows_of(chip(2 * sign))] += st1_in[h, 2].astype(F32)
        for slot, step in ((0, 2), (1, -2)):
            st2_out[h, slot] = (cp[h, rows_of(chip(step))] + st1_in[h, slot].astype(F32)).astype(BF16)
            scatter2(h, slot, step).start()

    def scatter_d(h):
        for slot in (3, 4):
            scatter1(h, slot, 1).wait_recv()
        for slot in (0, 1):
            scatter2(h, slot, 1).wait_recv()
        total = (
            cp[h, rows_of(z)] + st1_in[h, 3].astype(F32) + st1_in[h, 4].astype(F32)
            + st2_in[h, 0].astype(F32) + st2_in[h, 1].astype(F32)
        ).astype(BF16)
        dpk[:, column(h)] = total[:, :HEAD]
        dpv[:, column(h)] = total[:, HEAD:]

    token = lax.rem(lax.broadcasted_iota(jnp.int32, (1, WIDE), 1), ROWS)
    live = token < len_ref[me]
    causal = lax.broadcasted_iota(jnp.int32, (ROWS, WIDE), 0) <= lax.rem(
        lax.broadcasted_iota(jnp.int32, (ROWS, WIDE), 1), ROWS
    )
    ones = jnp.ones((8, HEAD), BF16)

    def column(h):
        return pl.ds(pl.multiple_of(h * HEAD, HEAD), HEAD)

    def two(ref, i):
        col = pl.multiple_of(i * WIDE, WIDE)
        return jnp.concatenate([ref[:, pl.ds(col, HEAD)], ref[:, pl.ds(col + HEAD, HEAD)]], axis=0)

    def prepare(i, _):
        q2, g2, o2 = two(q, i), two(g, i), two(o, i)
        product = g2.astype(F32) * o2.astype(F32)
        high = product.astype(BF16)
        low = (product - high.astype(F32)).astype(BF16)
        delta[i] = dot_nt(ones, high) + dot_nt(ones, low)
        col = column(i // PAIRS)
        rs_scr[i] = jnp.where(causal, dot_nt(rk[:, col], q2), -1e30)
        rdp_scr[i] = dot_nt(rv[:, col], g2)
        return 0

    gather_near(0)
    gather_near(1)
    for load in loads:
        load.wait()
    lax.fori_loop(0, GROUPS * PAIRS, prepare, 0)
    gather_far(0)
    gather_near(2)
    gather_far(1)
    gather_near(3)
    pass_on(0)

    def scores(h, p, state):
        i, b = h * PAIRS + p, p % 2
        q2 = two(q, i)

        def begin():
            state["top"] = fold(rs_scr[i], jnp.max)

        def step(r):
            rows = slice(r, r + BLOCK)
            s = dot_nt(kv[h, rows, :HEAD], q2)
            s_scr[b, rows] = s
            state["top"] = jnp.maximum(state["top"], fold(s, jnp.max))

        return [begin] + [functools.partial(step, r) for r in range(0, PROMPT, BLOCK)]

    def exponents(h, p, state):
        i, b = h * PAIRS + p, p % 2

        def begin():
            state["shift"] = jnp.max(state["top"], axis=0, keepdims=True) * SCALE2
            e = jnp.exp2(rs_scr[i] * SCALE2 - state["shift"])
            rs_scr[i] = e
            state["total"] = fold(e, jnp.sum)

        def step(r):
            rows = slice(r, r + BLOCK)
            e = jnp.exp2(s_scr[b, rows] * SCALE2 - state["shift"])
            s_scr[b, rows] = e
            state["total"] = state["total"] + fold(e, jnp.sum)

        return [begin] + [functools.partial(step, r) for r in range(0, PROMPT, BLOCK)]

    def score_grads(h, p, state):
        i, b = h * PAIRS + p, p % 2
        g2 = two(g, i)
        row_delta = delta[i][0:1]

        def begin():
            total = jnp.sum(state["total"], axis=0, keepdims=True)
            state["inverse"] = jnp.where(live, 1.0 / total, 0.0)
            probability = rs_scr[i] * state["inverse"]
            rp_scr[i] = probability.astype(BF16)
            ds_scr[i, PROMPT:] = (probability * (rdp_scr[i] - row_delta)).astype(BF16)

        def step(r):
            rows = slice(r, r + BLOCK)
            prob_grad = dot_nt(kv[h, rows, HEAD:], g2)
            probability = s_scr[b, rows] * state["inverse"]
            p_scr[p, rows] = probability.astype(BF16)
            ds_scr[i, rows] = (probability * (prob_grad - row_delta)).astype(BF16)

        return [begin] + [functools.partial(step, r) for r in range(0, PROMPT, BLOCK)]

    def prompt_grads(h, p):
        i = h * PAIRS + p

        def keys():
            a = dot(ds_scr[i, :PROMPT], two(q, i)) * SCALE
            acc[:, :HEAD] = a if p == 0 else acc[:, :HEAD] + a

        def values():
            a = dot(p_scr[p], two(g, i))
            acc[:, HEAD:] = a if p == 0 else acc[:, HEAD:] + a

        return [values, keys]

    def group(h, _):
        sib_gather(h, 1 - c).wait_recv()
        state, pending = {}, []
        for entry in scores(h, 0, state):
            entry()
        for p in range(PAIRS):
            following, ahead = {}, []
            if p + 1 < PAIRS:
                ahead = scores(h, p + 1, following)
            weave(exponents(h, p, state), ahead)
            weave(score_grads(h, p, state), pending)
            pending = prompt_grads(h, p)
            state = following
            if p < 2:
                @pl.when(h == 0)
                def _():
                    gather_far(2 + p)
            if p == 1:
                @pl.when(h >= 1)
                def _():
                    scatter_b(h - 1)

                @pl.when(h < GROUPS - 1)
                def _():
                    pass_on(h + 1)
            if p == 2:
                @pl.when(h >= 2)
                def _():
                    scatter_c(h - 2)
        for entry in pending:
            entry()
        scatter_a(h)
        return 0

    lax.fori_loop(0, GROUPS, group, 0)

    def finish_group(h, _):
        col = column(h)
        g8 = jnp.concatenate([two(g, h * PAIRS + p) for p in range(PAIRS)], axis=0)
        q8 = jnp.concatenate([two(q, h * PAIRS + p) for p in range(PAIRS)], axis=0)
        p8 = jnp.concatenate([rp_scr[h * PAIRS + p] for p in range(PAIRS)], axis=1)
        ds8 = jnp.concatenate([ds_scr[h * PAIRS + p, PROMPT:] for p in range(PAIRS)], axis=1)
        drv[:, col] = dot(p8, g8).astype(BF16)
        drk[:, col] = (dot(ds8, q8) * SCALE).astype(BF16)
        kt = jnp.concatenate([kv[h, :, :HEAD], rk[:, col]], axis=0).T
        for p in range(PAIRS):
            grad = dot(kt, ds_scr[h * PAIRS + p]) * SCALE
            at = pl.multiple_of((h * PAIRS + p) * WIDE, WIDE)
            dq[:, pl.ds(at, HEAD)] = grad[:, :ROWS].T.astype(BF16)
            dq[:, pl.ds(at + HEAD, HEAD)] = grad[:, ROWS:].T.astype(BF16)
        return 0

    def dq_out(i):
        cols = pl.ds(i * 2048, 2048)
        return pltpu.make_async_copy(dq.at[:, cols], dq_hbm.at[0, :, cols], out_sem.at[2 + i])

    out_rk = pltpu.make_async_copy(drk, drk_hbm.at[0], out_sem.at[0])
    out_rv = pltpu.make_async_copy(drv, drv_hbm.at[0], out_sem.at[1])
    out_pk = pltpu.make_async_copy(dpk, dpk_hbm, out_sem.at[4])
    out_pv = pltpu.make_async_copy(dpv, dpv_hbm, out_sem.at[5])
    lax.fori_loop(0, 2, finish_group, 0)
    dq_out(0).start()
    scatter_b(3)
    scatter_c(2)
    lax.fori_loop(2, 4, finish_group, 0)
    dq_out(1).start()
    out_rk.start()
    out_rv.start()
    scatter_d(0)
    scatter_d(1)

    def drain(h, _):
        for slot, step in near:
            gather(h, slot, 0, step).wait_send()
        gather(h, 4, -2, 1).wait_send()
        gather(h, 5, 2, -1).wait_send()
        gather(h, 6, -2 * sign, 2 * sign).wait_send()
        sib_gather(h, c).wait_send()
        sib_scatter(h).wait_send()
        return 0

    lax.fori_loop(0, GROUPS, drain, 0)
    scatter_c(3)
    scatter_d(2)
    scatter_d(3)
    out_pk.start()
    out_pv.start()

    def drain_scatter(h, _):
        for slot, step, owner in first:
            scatter1(h, slot, step).wait_send()
        scatter2(h, 0, 2).wait_send()
        scatter2(h, 1, -2).wait_send()
        return 0

    lax.fori_loop(0, GROUPS, drain_scatter, 0)
    for copy in (out_rk, out_rv, dq_out(0), dq_out(1), out_pk, out_pv):
        copy.wait()


def finish(*refs):
    sources, targets, held = refs[:5], refs[5:10], refs[10:15]
    in_sem, out_sem = refs[15:]
    parts = [(0, (slice(None), slice(None), pl.ds(part * 1024, 1024))) for part in range(4)]
    parts += [(i, ()) for i in range(1, 5)]

    def view(ref, index):
        return ref.at[index] if index else ref

    loads = [
        pltpu.make_async_copy(view(sources[i], at), view(held[i], at), in_sem.at[n])
        for n, (i, at) in enumerate(parts)
    ]
    stores = [
        pltpu.make_async_copy(view(held[i], at), view(targets[i], at), out_sem.at[n])
        for n, (i, at) in enumerate(parts)
    ]
    for load in loads:
        load.start()
    for load, store in zip(loads, stores):
        load.wait()
        store.start()
    for store in stores:
        store.wait()


def local(queries, outputs, out_grads, resp_keys, resp_values, lengths, prompt_keys, prompt_values):
    any_spec = pl.BlockSpec(memory_space=pl.ANY)
    pairs = GROUPS * PAIRS
    wide = (ROWS, pairs * WIDE)
    narrow = (ROWS, GROUPS * HEAD)
    block = (OWN, 2 * HEAD)
    half = (HALF, 2 * HEAD)
    shapes = [
        jax.ShapeDtypeStruct((1,) + wide, BF16),
        jax.ShapeDtypeStruct((1,) + narrow, BF16),
        jax.ShapeDtypeStruct((1,) + narrow, BF16),
        jax.ShapeDtypeStruct((OWN, GROUPS * HEAD), BF16),
        jax.ShapeDtypeStruct((OWN, GROUPS * HEAD), BF16),
    ]
    results = pl.pallas_call(
        kernel,
        name="grads",
        out_shape=shapes,
        in_specs=[any_spec] * 5 + [pl.BlockSpec(memory_space=pltpu.SMEM)] + [any_spec] * 2,
        out_specs=[any_spec] * 5,
        scratch_shapes=[
            pltpu.VMEM(wide, BF16),
            pltpu.VMEM(wide, BF16),
            pltpu.VMEM(wide, BF16),
            pltpu.VMEM(narrow, BF16),
            pltpu.VMEM(narrow, BF16),
            pltpu.VMEM((GROUPS, PROMPT, 2 * HEAD), BF16),
            pltpu.VMEM((2, PROMPT, WIDE), F32),
            pltpu.VMEM((pairs, ROWS, WIDE), F32),
            pltpu.VMEM((pairs, ROWS, WIDE), F32),
            pltpu.VMEM((PAIRS, PROMPT, WIDE), BF16),
            pltpu.VMEM((pairs, ROWS, WIDE), BF16),
            pltpu.VMEM((pairs, KEYS, WIDE), BF16),
            pltpu.VMEM((pairs, 8, WIDE), F32),
            pltpu.VMEM((PROMPT, 2 * HEAD), F32),
            pltpu.VMEM((GROUPS,) + half, F32),
            pltpu.VMEM((GROUPS,) + half, BF16),
            pltpu.VMEM((GROUPS,) + half, BF16),
            pltpu.VMEM((GROUPS, 5) + block, BF16),
            pltpu.VMEM((GROUPS, 5) + block, BF16),
            pltpu.VMEM((GROUPS, 2) + block, BF16),
            pltpu.VMEM((GROUPS, 2) + block, BF16),
            pltpu.VMEM(wide, BF16),
            pltpu.VMEM(narrow, BF16),
            pltpu.VMEM(narrow, BF16),
            pltpu.VMEM((OWN, GROUPS * HEAD), BF16),
            pltpu.VMEM((OWN, GROUPS * HEAD), BF16),
            pltpu.SemaphoreType.DMA((5,)),
            pltpu.SemaphoreType.DMA,
            pltpu.SemaphoreType.DMA((6,)),
            pltpu.SemaphoreType.DMA((GROUPS, 8)),
            pltpu.SemaphoreType.DMA((GROUPS, 8)),
            pltpu.SemaphoreType.DMA((GROUPS, 8)),
            pltpu.SemaphoreType.DMA((GROUPS, 8)),
        ],
        compiler_params=pltpu.CompilerParams(
            collective_id=0, has_side_effects=True, vmem_limit_bytes=56 * 2**20
        ),
        cost_estimate=pl.CostEstimate(flops=4700000000, bytes_accessed=5000000, transcendentals=3670016),
    )(queries, outputs, out_grads, resp_keys, resp_values, lengths, prompt_keys, prompt_values)
    return pl.pallas_call(
        finish,
        name="finish",
        out_shape=shapes,
        in_specs=[any_spec] * 5,
        out_specs=[any_spec] * 5,
        scratch_shapes=[pltpu.VMEM(shape.shape, shape.dtype) for shape in shapes]
        + [pltpu.SemaphoreType.DMA((8,))] * 2,
    )(*results)


def solution(mesh):
    rows = P(("dp", "seq"), None, None)
    prompt = P(("dp", "seq"), None)
    return jax.shard_map(
        local,
        mesh=mesh,
        in_specs=(rows, rows, rows, rows, rows, P("dp"), prompt, prompt),
        out_specs=(rows, rows, rows, prompt, prompt),
        check_vma=False,
    )
```

```python
import functools

import jax
import jax.numpy as jnp
from jax import lax
from jax.experimental import pallas as pl
from jax.experimental.pallas import tpu as pltpu
from jax.sharding import PartitionSpec as P

F32 = jnp.float32
BF16 = jnp.bfloat16
HEAD = 128
ROWS = 128
GROUPS = 4
PAIRS = 4
WIDE = 2 * ROWS
CHIPS = 8
OWN = 48
HALF = CHIPS * OWN
PROMPT = 2 * HALF
KEYS = PROMPT + ROWS
BLOCK = 256
SCALE = HEAD**-0.5
SCALE2 = SCALE * 1.4426950408889634
MESH = pl.DeviceIdType.MESH


def dot(a, b):
    return jnp.dot(a, b, preferred_element_type=F32)


def dot_nt(a, b):
    return lax.dot_general(a, b, (((1,), (1,)), ((), ())), preferred_element_type=F32)


def fold(x, op):
    return op(x.reshape(x.shape[0] // 8, 8, x.shape[1]), axis=0)


def weave(*lists):
    steps = max(len(entry) for entry in lists)
    done = [0] * len(lists)
    for step in range(steps):
        for i, entry in enumerate(lists):
            while done[i] < len(entry) and done[i] * steps < (step + 1) * len(entry):
                entry[done[i]]()
                done[i] += 1


def kernel(
    q_hbm, o_hbm, g_hbm, rk_hbm, rv_hbm, len_hbm, pk_hbm, pv_hbm,
    dq_hbm, drk_hbm, drv_hbm, dpk_hbm, dpv_hbm,
    q, o, g, rk, rv, kv, s_scr, rs_scr, rdp_scr, p_scr, rp_scr, ds_scr, delta, acc, cp,
    sib_out, sib_in, st1_out, st1_in, st2_out, st2_in, dq, drk, drv, dpk, dpv,
    len_ref, in_sem, own_sem, out_sem, gs_sem, gr_sem, ss_sem, sr_sem,
):
    me = lax.axis_index("seq")
    z = me // 2
    c = lax.rem(me, 2)
    sign = 1 - 2 * c
    sibling = me + sign

    def chip(k):
        return lax.rem(z + k + 16, CHIPS)

    def device(k):
        return chip(k) * 2 + c

    def rows_of(zz):
        return pl.ds(pl.multiple_of(zz * OWN, 16), OWN)

    def half_of(core):
        return pl.ds(pl.multiple_of(core * HALF, HALF), HALF)

    def block_of(zz):
        return pl.ds(pl.multiple_of((c * CHIPS + zz) * OWN, 16), OWN)

    loads = []
    for i, (src, dst) in enumerate(((g_hbm, g), (o_hbm, o), (q_hbm, q), (rk_hbm, rk), (rv_hbm, rv))):
        loads.append(pltpu.make_async_copy(src.at[0], dst, in_sem.at[i]))
    loads.append(pltpu.make_async_copy(len_hbm, len_ref, in_sem.at[5]))
    own = kv.at[:, block_of(z)]
    for h in range(GROUPS):
        cols = pl.ds(h * HEAD, HEAD)
        pltpu.make_async_copy(pk_hbm.at[:, cols], kv.at[h, block_of(z), pl.ds(0, HEAD)], own_sem).start()
        pltpu.make_async_copy(pv_hbm.at[:, cols], kv.at[h, block_of(z), pl.ds(HEAD, HEAD)], own_sem).start()
    for load in loads:
        load.start()

    barrier = pltpu.get_barrier_semaphore()
    for target in (device(1), device(-1), device(2), device(-2), sibling):
        pl.semaphore_signal(barrier, inc=1, device_id={"seq": target}, device_id_type=MESH)
    pl.semaphore_wait(barrier, 5)
    pltpu.make_async_copy(own, own, own_sem).wait()

    def remote(src, dst, send, recv, target):
        return pltpu.make_async_remote_copy(
            src_ref=src, dst_ref=dst, send_sem=send, recv_sem=recv,
            device_id={"seq": target}, device_id_type=MESH,
        )

    def gather(h, slot, origin, target):
        block = kv.at[h, block_of(chip(origin))]
        return remote(block, block, gs_sem.at[h, slot], gr_sem.at[h, slot], device(target))

    def gather_wait(h, slot, origin):
        gather(h, slot, origin, 1).wait_recv()

    near = ((2, 2), (3, -2), (0, 1), (1, -1))

    def gather_near(h):
        for slot, step in near:
            gather(h, slot, 0, step).start()

    def gather_far(h):
        gather_wait(h, 2, -2)
        gather(h, 4, -2, 1).start()
        gather_wait(h, 3, 2)
        gather(h, 5, 2, -1).start()
        gather(h, 6, -2 * sign, 2 * sign).start()

    def sib_gather(h, core):
        part = kv.at[h, half_of(core)]
        return remote(part, part, gs_sem.at[h, 7], gr_sem.at[h, 7], sibling)

    def pass_on(h):
        for slot, origin in ((0, -1), (1, 1), (4, -3), (5, 3), (6, 4)):
            gather_wait(h, slot, origin)
        sib_gather(h, c).start()

    def sib_scatter(h):
        return remote(sib_out.at[h], sib_in.at[h], ss_sem.at[h, 0], sr_sem.at[h, 0], sibling)

    def scatter1(h, slot, step):
        return remote(
            st1_out.at[h, slot], st1_in.at[h, slot], ss_sem.at[h, 1 + slot], sr_sem.at[h, 1 + slot], device(step)
        )

    def scatter2(h, slot, step):
        return remote(
            st2_out.at[h, slot], st2_in.at[h, slot], ss_sem.at[h, 6 + slot], sr_sem.at[h, 6 + slot], device(step)
        )

    first = ((0, 1, 3), (1, -1, -3), (2, 2 * sign, 4), (3, 1, 1), (4, -1, -1))

    def scatter_a(h):
        sib_out[h] = acc[half_of(1 - c)].astype(BF16)
        sib_scatter(h).start()
        cp[h] = acc[half_of(c)]

    def scatter_b(h):
        sib_scatter(h).wait_recv()
        cp[h] += sib_in[h].astype(F32)
        for slot, step, owner in first:
            st1_out[h, slot] = cp[h, rows_of(chip(owner))].astype(BF16)
            scatter1(h, slot, step).start()

    def scatter_c(h):
        for slot in range(3):
            scatter1(h, slot, 1).wait_recv()
        cp[h, rows_of(chip(2 * sign))] += st1_in[h, 2].astype(F32)
        for slot, step in ((0, 2), (1, -2)):
            st2_out[h, slot] = (cp[h, rows_of(chip(step))] + st1_in[h, slot].astype(F32)).astype(BF16)
            scatter2(h, slot, step).start()

    def scatter_d(h):
        for slot in (3, 4):
            scatter1(h, slot, 1).wait_recv()
        for slot in (0, 1):
            scatter2(h, slot, 1).wait_recv()
        total = (
            cp[h, rows_of(z)] + st1_in[h, 3].astype(F32) + st1_in[h, 4].astype(F32)
            + st2_in[h, 0].astype(F32) + st2_in[h, 1].astype(F32)
        ).astype(BF16)
        dpk[:, column(h)] = total[:, :HEAD]
        dpv[:, column(h)] = total[:, HEAD:]

    token = lax.rem(lax.broadcasted_iota(jnp.int32, (1, WIDE), 1), ROWS)
    causal = lax.broadcasted_iota(jnp.int32, (ROWS, WIDE), 0) <= lax.rem(
        lax.broadcasted_iota(jnp.int32, (ROWS, WIDE), 1), ROWS
    )
    ones = jnp.ones((8, HEAD), BF16)

    def column(h):
        return pl.ds(pl.multiple_of(h * HEAD, HEAD), HEAD)

    def two(ref, i):
        col = pl.multiple_of(i * WIDE, WIDE)
        return jnp.concatenate([ref[:, pl.ds(col, HEAD)], ref[:, pl.ds(col + HEAD, HEAD)]], axis=0)

    def prepare(i, _):
        q2, g2, o2 = two(q, i), two(g, i), two(o, i)
        product = g2.astype(F32) * o2.astype(F32)
        high = product.astype(BF16)
        low = (product - high.astype(F32)).astype(BF16)
        delta[i] = dot_nt(ones, high) + dot_nt(ones, low)
        col = column(i // PAIRS)
        rs_scr[i] = jnp.where(causal, dot_nt(rk[:, col], q2), -1e30)
        rdp_scr[i] = dot_nt(rv[:, col], g2)
        return 0

    gather_near(0)
    gather_near(1)
    for load in loads:
        load.wait()
    lax.fori_loop(0, GROUPS * PAIRS, prepare, 0)
    gather_far(0)
    gather_near(2)
    gather_far(1)
    gather_near(3)
    pass_on(0)

    live = token < len_ref[me]

    def scores(h, p, state):
        i, b = h * PAIRS + p, p % 2
        q2 = two(q, i)

        def begin():
            state["top"] = fold(rs_scr[i], jnp.max)

        def step(r):
            rows = slice(r, r + BLOCK)
            s = dot_nt(kv[h, rows, :HEAD], q2)
            s_scr[b, rows] = s
            state["top"] = jnp.maximum(state["top"], fold(s, jnp.max))

        return [begin] + [functools.partial(step, r) for r in range(0, PROMPT, BLOCK)]

    def exponents(h, p, state):
        i, b = h * PAIRS + p, p % 2

        def begin():
            state["shift"] = jnp.max(state["top"], axis=0, keepdims=True) * SCALE2
            e = jnp.exp2(rs_scr[i] * SCALE2 - state["shift"])
            rs_scr[i] = e
            state["total"] = fold(e, jnp.sum)

        def step(r):
            rows = slice(r, r + BLOCK)
            e = jnp.exp2(s_scr[b, rows] * SCALE2 - state["shift"])
            s_scr[b, rows] = e
            state["total"] = state["total"] + fold(e, jnp.sum)

        return [begin] + [functools.partial(step, r) for r in range(0, PROMPT, BLOCK)]

    def score_grads(h, p, state):
        i, b = h * PAIRS + p, p % 2
        g2 = two(g, i)
        row_delta = delta[i][0:1]

        def begin():
            total = jnp.sum(state["total"], axis=0, keepdims=True)
            state["inverse"] = jnp.where(live, 1.0 / total, 0.0)
            probability = rs_scr[i] * state["inverse"]
            rp_scr[i] = probability.astype(BF16)
            ds_scr[i, PROMPT:] = (probability * (rdp_scr[i] - row_delta)).astype(BF16)

        def step(r):
            rows = slice(r, r + BLOCK)
            prob_grad = dot_nt(kv[h, rows, HEAD:], g2)
            probability = s_scr[b, rows] * state["inverse"]
            p_scr[p, rows] = probability.astype(BF16)
            ds_scr[i, rows] = (probability * (prob_grad - row_delta)).astype(BF16)

        return [begin] + [functools.partial(step, r) for r in range(0, PROMPT, BLOCK)]

    def prompt_grads(h, p):
        i = h * PAIRS + p

        def keys():
            a = dot(ds_scr[i, :PROMPT], two(q, i)) * SCALE
            acc[:, :HEAD] = a if p == 0 else acc[:, :HEAD] + a

        def values():
            a = dot(p_scr[p], two(g, i))
            acc[:, HEAD:] = a if p == 0 else acc[:, HEAD:] + a

        return [values, keys]

    def group(h, _):
        sib_gather(h, 1 - c).wait_recv()
        state, pending = {}, []
        for entry in scores(h, 0, state):
            entry()
        for p in range(PAIRS):
            following, ahead = {}, []
            if p + 1 < PAIRS:
                ahead = scores(h, p + 1, following)
            weave(exponents(h, p, state), ahead)
            weave(score_grads(h, p, state), pending)
            pending = prompt_grads(h, p)
            state = following
            if p < 2:
                @pl.when(h == 0)
                def _():
                    gather_far(2 + p)
            if p == 1:
                @pl.when(h >= 1)
                def _():
                    scatter_b(h - 1)

                @pl.when(h < GROUPS - 1)
                def _():
                    pass_on(h + 1)
            if p == 2:
                @pl.when(h >= 2)
                def _():
                    scatter_c(h - 2)
        for entry in pending:
            entry()
        scatter_a(h)
        return 0

    lax.fori_loop(0, GROUPS, group, 0)

    def finish_group(h, _):
        col = column(h)
        g8 = jnp.concatenate([two(g, h * PAIRS + p) for p in range(PAIRS)], axis=0)
        q8 = jnp.concatenate([two(q, h * PAIRS + p) for p in range(PAIRS)], axis=0)
        p8 = jnp.concatenate([rp_scr[h * PAIRS + p] for p in range(PAIRS)], axis=1)
        ds8 = jnp.concatenate([ds_scr[h * PAIRS + p, PROMPT:] for p in range(PAIRS)], axis=1)
        drv[:, col] = dot(p8, g8).astype(BF16)
        drk[:, col] = (dot(ds8, q8) * SCALE).astype(BF16)
        kt = jnp.concatenate([kv[h, :, :HEAD], rk[:, col]], axis=0).T
        for p in range(PAIRS):
            grad = dot(kt, ds_scr[h * PAIRS + p]) * SCALE
            at = pl.multiple_of((h * PAIRS + p) * WIDE, WIDE)
            dq[:, pl.ds(at, HEAD)] = grad[:, :ROWS].T.astype(BF16)
            dq[:, pl.ds(at + HEAD, HEAD)] = grad[:, ROWS:].T.astype(BF16)
        return 0

    def dq_out(i):
        cols = pl.ds(i * 2048, 2048)
        return pltpu.make_async_copy(dq.at[:, cols], dq_hbm.at[0, :, cols], out_sem.at[2 + i])

    out_rk = pltpu.make_async_copy(drk, drk_hbm.at[0], out_sem.at[0])
    out_rv = pltpu.make_async_copy(drv, drv_hbm.at[0], out_sem.at[1])
    out_pk = pltpu.make_async_copy(dpk, dpk_hbm, out_sem.at[4])
    out_pv = pltpu.make_async_copy(dpv, dpv_hbm, out_sem.at[5])
    lax.fori_loop(0, 2, finish_group, 0)
    dq_out(0).start()
    scatter_b(3)
    lax.fori_loop(2, 4, finish_group, 0)
    scatter_c(2)
    dq_out(1).start()
    out_rk.start()
    out_rv.start()
    scatter_d(0)
    scatter_d(1)

    def drain(h, _):
        for slot, step in near:
            gather(h, slot, 0, step).wait_send()
        gather(h, 4, -2, 1).wait_send()
        gather(h, 5, 2, -1).wait_send()
        gather(h, 6, -2 * sign, 2 * sign).wait_send()
        sib_gather(h, c).wait_send()
        sib_scatter(h).wait_send()
        return 0

    lax.fori_loop(0, GROUPS, drain, 0)
    scatter_c(3)
    scatter_d(2)
    scatter_d(3)
    out_pk.start()
    out_pv.start()

    def drain_scatter(h, _):
        for slot, step, owner in first:
            scatter1(h, slot, step).wait_send()
        scatter2(h, 0, 2).wait_send()
        scatter2(h, 1, -2).wait_send()
        return 0

    lax.fori_loop(0, GROUPS, drain_scatter, 0)
    for copy in (out_rk, out_rv, dq_out(0), dq_out(1), out_pk, out_pv):
        copy.wait()


def finish(*refs):
    sources, targets, held = refs[:5], refs[5:10], refs[10:15]
    in_sem, out_sem = refs[15:]
    parts = [(0, (slice(None), slice(None), pl.ds(part * 1024, 1024))) for part in range(4)]
    parts += [(i, ()) for i in range(1, 5)]

    def view(ref, index):
        return ref.at[index] if index else ref

    loads = [
        pltpu.make_async_copy(view(sources[i], at), view(held[i], at), in_sem.at[n])
        for n, (i, at) in enumerate(parts)
    ]
    stores = [
        pltpu.make_async_copy(view(held[i], at), view(targets[i], at), out_sem.at[n])
        for n, (i, at) in enumerate(parts)
    ]
    for load in loads:
        load.start()
    for load, store in zip(loads, stores):
        load.wait()
        store.start()
    for store in stores:
        store.wait()


def local(queries, outputs, out_grads, resp_keys, resp_values, lengths, prompt_keys, prompt_values):
    any_spec = pl.BlockSpec(memory_space=pl.ANY)
    pairs = GROUPS * PAIRS
    wide = (ROWS, pairs * WIDE)
    narrow = (ROWS, GROUPS * HEAD)
    block = (OWN, 2 * HEAD)
    half = (HALF, 2 * HEAD)
    shapes = [
        jax.ShapeDtypeStruct((1,) + wide, BF16),
        jax.ShapeDtypeStruct((1,) + narrow, BF16),
        jax.ShapeDtypeStruct((1,) + narrow, BF16),
        jax.ShapeDtypeStruct((OWN, GROUPS * HEAD), BF16),
        jax.ShapeDtypeStruct((OWN, GROUPS * HEAD), BF16),
    ]
    results = pl.pallas_call(
        kernel,
        name="grads",
        out_shape=shapes,
        in_specs=[any_spec] * 8,
        out_specs=[any_spec] * 5,
        scratch_shapes=[
            pltpu.VMEM(wide, BF16),
            pltpu.VMEM(wide, BF16),
            pltpu.VMEM(wide, BF16),
            pltpu.VMEM(narrow, BF16),
            pltpu.VMEM(narrow, BF16),
            pltpu.VMEM((GROUPS, PROMPT, 2 * HEAD), BF16),
            pltpu.VMEM((2, PROMPT, WIDE), F32),
            pltpu.VMEM((pairs, ROWS, WIDE), F32),
            pltpu.VMEM((pairs, ROWS, WIDE), F32),
            pltpu.VMEM((PAIRS, PROMPT, WIDE), BF16),
            pltpu.VMEM((pairs, ROWS, WIDE), BF16),
            pltpu.VMEM((pairs, KEYS, WIDE), BF16),
            pltpu.VMEM((pairs, 8, WIDE), F32),
            pltpu.VMEM((PROMPT, 2 * HEAD), F32),
            pltpu.VMEM((GROUPS,) + half, F32),
            pltpu.VMEM((GROUPS,) + half, BF16),
            pltpu.VMEM((GROUPS,) + half, BF16),
            pltpu.VMEM((GROUPS, 5) + block, BF16),
            pltpu.VMEM((GROUPS, 5) + block, BF16),
            pltpu.VMEM((GROUPS, 2) + block, BF16),
            pltpu.VMEM((GROUPS, 2) + block, BF16),
            pltpu.VMEM(wide, BF16),
            pltpu.VMEM(narrow, BF16),
            pltpu.VMEM(narrow, BF16),
            pltpu.VMEM((OWN, GROUPS * HEAD), BF16),
            pltpu.VMEM((OWN, GROUPS * HEAD), BF16),
            pltpu.SMEM((2 * CHIPS,), jnp.int32),
            pltpu.SemaphoreType.DMA((6,)),
            pltpu.SemaphoreType.DMA,
            pltpu.SemaphoreType.DMA((6,)),
            pltpu.SemaphoreType.DMA((GROUPS, 8)),
            pltpu.SemaphoreType.DMA((GROUPS, 8)),
            pltpu.SemaphoreType.DMA((GROUPS, 8)),
            pltpu.SemaphoreType.DMA((GROUPS, 8)),
        ],
        compiler_params=pltpu.CompilerParams(
            collective_id=0, has_side_effects=True, vmem_limit_bytes=56 * 2**20
        ),
        cost_estimate=pl.CostEstimate(flops=4700000000, bytes_accessed=5000000, transcendentals=3670016),
    )(queries, outputs, out_grads, resp_keys, resp_values, lengths, prompt_keys, prompt_values)
    return pl.pallas_call(
        finish,
        name="finish",
        out_shape=shapes,
        in_specs=[any_spec] * 5,
        out_specs=[any_spec] * 5,
        scratch_shapes=[pltpu.VMEM(shape.shape, shape.dtype) for shape in shapes]
        + [pltpu.SemaphoreType.DMA((8,))] * 2,
    )(*results)


def solution(mesh):
    rows = P(("dp", "seq"), None, None)
    prompt = P(("dp", "seq"), None)
    return jax.shard_map(
        local,
        mesh=mesh,
        in_specs=(rows, rows, rows, rows, rows, P("dp"), prompt, prompt),
        out_specs=(rows, rows, rows, prompt, prompt),
        check_vma=False,
    )
```

```python
import functools

import jax
import jax.numpy as jnp
from jax import lax
from jax.experimental import pallas as pl
from jax.experimental.pallas import tpu as pltpu
from jax.sharding import PartitionSpec as P

F32 = jnp.float32
BF16 = jnp.bfloat16
HEAD = 128
ROWS = 128
GROUPS = 4
PAIRS = 4
WIDE = 2 * ROWS
CHIPS = 8
OWN = 48
HALF = CHIPS * OWN
PROMPT = 2 * HALF
KEYS = PROMPT + ROWS
BLOCK = 256
SCALE = HEAD**-0.5
SCALE2 = SCALE * 1.4426950408889634
MESH = pl.DeviceIdType.MESH


def dot(a, b):
    return jnp.dot(a, b, preferred_element_type=F32)


def dot_nt(a, b):
    return lax.dot_general(a, b, (((1,), (1,)), ((), ())), preferred_element_type=F32)


def fold(x, op):
    return op(x.reshape(x.shape[0] // 8, 8, x.shape[1]), axis=0)


def weave(*lists):
    steps = max(len(entry) for entry in lists)
    done = [0] * len(lists)
    for step in range(steps):
        for i, entry in enumerate(lists):
            while done[i] < len(entry) and done[i] * steps < (step + 1) * len(entry):
                entry[done[i]]()
                done[i] += 1


def kernel(
    q_hbm, o_hbm, g_hbm, rk_hbm, rv_hbm, len_hbm, pk_hbm, pv_hbm,
    dq_hbm, drk_hbm, drv_hbm, dpk_hbm, dpv_hbm,
    q, o, g, rk, rv, kv, s_scr, rs_scr, rdp_scr, p_scr, rp_scr, ds_scr, delta, acc, cp,
    sib_out, sib_in, st1_out, st1_in, st2_out, st2_in, dq, drk, drv, dpk, dpv,
    len_ref, in_sem, own_sem, out_sem, gs_sem, gr_sem, ss_sem, sr_sem,
):
    me = lax.axis_index("seq")
    z = me // 2
    c = lax.rem(me, 2)
    sign = 1 - 2 * c
    sibling = me + sign

    def chip(k):
        return lax.rem(z + k + 16, CHIPS)

    def device(k):
        return chip(k) * 2 + c

    def rows_of(zz):
        return pl.ds(pl.multiple_of(zz * OWN, 16), OWN)

    def half_of(core):
        return pl.ds(pl.multiple_of(core * HALF, HALF), HALF)

    def block_of(zz):
        return pl.ds(pl.multiple_of((c * CHIPS + zz) * OWN, 16), OWN)

    loads = []
    for i, (src, dst) in enumerate(((g_hbm, g), (o_hbm, o), (q_hbm, q), (rk_hbm, rk), (rv_hbm, rv))):
        loads.append(pltpu.make_async_copy(src.at[0], dst, in_sem.at[i]))
    loads.append(pltpu.make_async_copy(len_hbm, len_ref, in_sem.at[5]))
    own = kv.at[:, block_of(z)]
    for h in range(GROUPS):
        cols = pl.ds(h * HEAD, HEAD)
        pltpu.make_async_copy(pk_hbm.at[:, cols], kv.at[h, block_of(z), pl.ds(0, HEAD)], own_sem).start()
        pltpu.make_async_copy(pv_hbm.at[:, cols], kv.at[h, block_of(z), pl.ds(HEAD, HEAD)], own_sem).start()
    for load in loads:
        load.start()

    barrier = pltpu.get_barrier_semaphore()
    for target in (device(1), device(-1), device(2), device(-2), sibling):
        pl.semaphore_signal(barrier, inc=1, device_id={"seq": target}, device_id_type=MESH)
    pl.semaphore_wait(barrier, 5)
    pltpu.make_async_copy(own, own, own_sem).wait()

    def remote(src, dst, send, recv, target):
        return pltpu.make_async_remote_copy(
            src_ref=src, dst_ref=dst, send_sem=send, recv_sem=recv,
            device_id={"seq": target}, device_id_type=MESH,
        )

    def gather(h, slot, origin, target):
        block = kv.at[h, block_of(chip(origin))]
        return remote(block, block, gs_sem.at[h, slot], gr_sem.at[h, slot], device(target))

    def gather_wait(h, slot, origin):
        gather(h, slot, origin, 1).wait_recv()

    near = ((2, 2), (3, -2), (0, 1), (1, -1))

    def gather_near(h):
        for slot, step in near:
            gather(h, slot, 0, step).start()

    def gather_far(h):
        gather_wait(h, 2, -2)
        gather(h, 4, -2, 1).start()
        gather_wait(h, 3, 2)
        gather(h, 5, 2, -1).start()
        gather(h, 6, -2 * sign, 2 * sign).start()

    def sib_gather(h, core):
        part = kv.at[h, half_of(core)]
        return remote(part, part, gs_sem.at[h, 7], gr_sem.at[h, 7], sibling)

    def pass_on(h):
        for slot, origin in ((0, -1), (1, 1), (4, -3), (5, 3), (6, 4)):
            gather_wait(h, slot, origin)
        sib_gather(h, c).start()

    def sib_scatter(h):
        return remote(sib_out.at[h], sib_in.at[h], ss_sem.at[h, 0], sr_sem.at[h, 0], sibling)

    def scatter1(h, slot, step):
        return remote(
            st1_out.at[h, slot], st1_in.at[h, slot], ss_sem.at[h, 1 + slot], sr_sem.at[h, 1 + slot], device(step)
        )

    def scatter2(h, slot, step):
        return remote(
            st2_out.at[h, slot], st2_in.at[h, slot], ss_sem.at[h, 6 + slot], sr_sem.at[h, 6 + slot], device(step)
        )

    first = ((0, 1, 3), (1, -1, -3), (2, 2 * sign, 4), (3, 1, 1), (4, -1, -1))

    def scatter_a(h):
        i = h * PAIRS + PAIRS - 1

        def summed(core):
            rows = half_of(core)
            value = dot(p_scr[PAIRS - 1, rows], two(g, i))
            key = dot(ds_scr[i, rows], two(q, i)) * SCALE
            return acc[rows] + jnp.concatenate([key, value], axis=1)

        sib_out[h] = summed(1 - c).astype(BF16)
        sib_scatter(h).start()
        cp[h] = summed(c)

    def scatter_b(h):
        sib_scatter(h).wait_recv()
        cp[h] += sib_in[h].astype(F32)
        for slot, step, owner in first:
            st1_out[h, slot] = cp[h, rows_of(chip(owner))].astype(BF16)
            scatter1(h, slot, step).start()

    def scatter_c(h):
        for slot in range(3):
            scatter1(h, slot, 1).wait_recv()
        cp[h, rows_of(chip(2 * sign))] += st1_in[h, 2].astype(F32)
        for slot, step in ((0, 2), (1, -2)):
            st2_out[h, slot] = (cp[h, rows_of(chip(step))] + st1_in[h, slot].astype(F32)).astype(BF16)
            scatter2(h, slot, step).start()

    def scatter_d(h):
        for slot in (3, 4):
            scatter1(h, slot, 1).wait_recv()
        for slot in (0, 1):
            scatter2(h, slot, 1).wait_recv()
        total = (
            cp[h, rows_of(z)] + st1_in[h, 3].astype(F32) + st1_in[h, 4].astype(F32)
            + st2_in[h, 0].astype(F32) + st2_in[h, 1].astype(F32)
        ).astype(BF16)
        dpk[:, column(h)] = total[:, :HEAD]
        dpv[:, column(h)] = total[:, HEAD:]

    token = lax.rem(lax.broadcasted_iota(jnp.int32, (1, WIDE), 1), ROWS)
    causal = lax.broadcasted_iota(jnp.int32, (ROWS, WIDE), 0) <= lax.rem(
        lax.broadcasted_iota(jnp.int32, (ROWS, WIDE), 1), ROWS
    )
    ones = jnp.ones((8, HEAD), BF16)

    def column(h):
        return pl.ds(pl.multiple_of(h * HEAD, HEAD), HEAD)

    def two(ref, i):
        col = pl.multiple_of(i * WIDE, WIDE)
        return jnp.concatenate([ref[:, pl.ds(col, HEAD)], ref[:, pl.ds(col + HEAD, HEAD)]], axis=0)

    def prepare(i, _):
        q2, g2, o2 = two(q, i), two(g, i), two(o, i)
        product = g2.astype(F32) * o2.astype(F32)
        high = product.astype(BF16)
        low = (product - high.astype(F32)).astype(BF16)
        delta[i] = dot_nt(ones, high) + dot_nt(ones, low)
        col = column(i // PAIRS)
        rs_scr[i] = jnp.where(causal, dot_nt(rk[:, col], q2), -1e30)
        rdp_scr[i] = dot_nt(rv[:, col], g2)
        return 0

    gather_near(0)
    gather_near(1)
    for load in loads:
        load.wait()
    lax.fori_loop(0, GROUPS * PAIRS, prepare, 0)
    gather_far(0)
    gather_near(2)
    gather_far(1)
    gather_near(3)
    pass_on(0)

    live = token < len_ref[me]

    def scores(h, p, state):
        i, b = h * PAIRS + p, p % 2
        q2 = two(q, i)

        def begin():
            state["top"] = fold(rs_scr[i], jnp.max)

        def step(r):
            rows = slice(r, r + BLOCK)
            s = dot_nt(kv[h, rows, :HEAD], q2)
            s_scr[b, rows] = s
            state["top"] = jnp.maximum(state["top"], fold(s, jnp.max))

        return [begin] + [functools.partial(step, r) for r in range(0, PROMPT, BLOCK)]

    def exponents(h, p, state):
        i, b = h * PAIRS + p, p % 2

        def begin():
            state["shift"] = jnp.max(state["top"], axis=0, keepdims=True) * SCALE2
            e = jnp.exp2(rs_scr[i] * SCALE2 - state["shift"])
            rs_scr[i] = e
            state["total"] = fold(e, jnp.sum)

        def step(r):
            rows = slice(r, r + BLOCK)
            e = jnp.exp2(s_scr[b, rows] * SCALE2 - state["shift"])
            s_scr[b, rows] = e
            state["total"] = state["total"] + fold(e, jnp.sum)

        return [begin] + [functools.partial(step, r) for r in range(0, PROMPT, BLOCK)]

    def score_grads(h, p, state):
        i, b = h * PAIRS + p, p % 2
        g2 = two(g, i)
        row_delta = delta[i][0:1]

        def begin():
            total = jnp.sum(state["total"], axis=0, keepdims=True)
            state["inverse"] = jnp.where(live, 1.0 / total, 0.0)
            probability = rs_scr[i] * state["inverse"]
            rp_scr[i] = probability.astype(BF16)
            ds_scr[i, PROMPT:] = (probability * (rdp_scr[i] - row_delta)).astype(BF16)

        def step(r):
            rows = slice(r, r + BLOCK)
            prob_grad = dot_nt(kv[h, rows, HEAD:], g2)
            probability = s_scr[b, rows] * state["inverse"]
            p_scr[p, rows] = probability.astype(BF16)
            ds_scr[i, rows] = (probability * (prob_grad - row_delta)).astype(BF16)

        return [begin] + [functools.partial(step, r) for r in range(0, PROMPT, BLOCK)]

    def prompt_grads(h, p):
        i = h * PAIRS + p

        def keys():
            a = dot(ds_scr[i, :PROMPT], two(q, i)) * SCALE
            acc[:, :HEAD] = a if p == 0 else acc[:, :HEAD] + a

        def values():
            a = dot(p_scr[p], two(g, i))
            acc[:, HEAD:] = a if p == 0 else acc[:, HEAD:] + a

        return [values, keys]

    def group(h, _):
        sib_gather(h, 1 - c).wait_recv()
        state, pending = {}, []
        for entry in scores(h, 0, state):
            entry()
        for p in range(PAIRS):
            following, ahead = {}, []
            if p + 1 < PAIRS:
                ahead = scores(h, p + 1, following)
            weave(exponents(h, p, state), ahead)
            weave(score_grads(h, p, state), pending)
            pending = prompt_grads(h, p) if p + 1 < PAIRS else []
            state = following
            if p < 2:
                @pl.when(h == 0)
                def _():
                    gather_far(2 + p)
            if p == 1:
                @pl.when(h >= 1)
                def _():
                    scatter_b(h - 1)

                @pl.when(h < GROUPS - 1)
                def _():
                    pass_on(h + 1)
            if p == 2:
                @pl.when(h >= 2)
                def _():
                    scatter_c(h - 2)
        scatter_a(h)
        return 0

    lax.fori_loop(0, GROUPS, group, 0)

    def finish_group(h, _):
        col = column(h)
        g8 = jnp.concatenate([two(g, h * PAIRS + p) for p in range(PAIRS)], axis=0)
        q8 = jnp.concatenate([two(q, h * PAIRS + p) for p in range(PAIRS)], axis=0)
        p8 = jnp.concatenate([rp_scr[h * PAIRS + p] for p in range(PAIRS)], axis=1)
        ds8 = jnp.concatenate([ds_scr[h * PAIRS + p, PROMPT:] for p in range(PAIRS)], axis=1)
        drv[:, col] = dot(p8, g8).astype(BF16)
        drk[:, col] = (dot(ds8, q8) * SCALE).astype(BF16)
        kt = jnp.concatenate([kv[h, :, :HEAD], rk[:, col]], axis=0).T
        for p in range(PAIRS):
            grad = dot(kt, ds_scr[h * PAIRS + p]) * SCALE
            at = pl.multiple_of((h * PAIRS + p) * WIDE, WIDE)
            dq[:, pl.ds(at, HEAD)] = grad[:, :ROWS].T.astype(BF16)
            dq[:, pl.ds(at + HEAD, HEAD)] = grad[:, ROWS:].T.astype(BF16)
        return 0

    def dq_out(i):
        cols = pl.ds(i * 2048, 2048)
        return pltpu.make_async_copy(dq.at[:, cols], dq_hbm.at[0, :, cols], out_sem.at[2 + i])

    out_rk = pltpu.make_async_copy(drk, drk_hbm.at[0], out_sem.at[0])
    out_rv = pltpu.make_async_copy(drv, drv_hbm.at[0], out_sem.at[1])
    out_pk = pltpu.make_async_copy(dpk, dpk_hbm, out_sem.at[4])
    out_pv = pltpu.make_async_copy(dpv, dpv_hbm, out_sem.at[5])
    lax.fori_loop(0, 2, finish_group, 0)
    dq_out(0).start()
    scatter_b(3)
    lax.fori_loop(2, 4, finish_group, 0)
    scatter_c(2)
    dq_out(1).start()
    out_rk.start()
    out_rv.start()
    scatter_d(0)
    scatter_d(1)

    def drain(h, _):
        for slot, step in near:
            gather(h, slot, 0, step).wait_send()
        gather(h, 4, -2, 1).wait_send()
        gather(h, 5, 2, -1).wait_send()
        gather(h, 6, -2 * sign, 2 * sign).wait_send()
        sib_gather(h, c).wait_send()
        sib_scatter(h).wait_send()
        return 0

    lax.fori_loop(0, GROUPS, drain, 0)
    scatter_c(3)
    scatter_d(2)
    scatter_d(3)
    out_pk.start()
    out_pv.start()

    def drain_scatter(h, _):
        for slot, step, owner in first:
            scatter1(h, slot, step).wait_send()
        scatter2(h, 0, 2).wait_send()
        scatter2(h, 1, -2).wait_send()
        return 0

    lax.fori_loop(0, GROUPS, drain_scatter, 0)
    for copy in (out_rk, out_rv, dq_out(0), dq_out(1), out_pk, out_pv):
        copy.wait()


def finish(*refs):
    sources, targets, held = refs[:5], refs[5:10], refs[10:15]
    in_sem, out_sem = refs[15:]
    parts = [(0, (slice(None), slice(None), pl.ds(part * 1024, 1024))) for part in range(4)]
    parts += [(i, ()) for i in range(1, 5)]

    def view(ref, index):
        return ref.at[index] if index else ref

    loads = [
        pltpu.make_async_copy(view(sources[i], at), view(held[i], at), in_sem.at[n])
        for n, (i, at) in enumerate(parts)
    ]
    stores = [
        pltpu.make_async_copy(view(held[i], at), view(targets[i], at), out_sem.at[n])
        for n, (i, at) in enumerate(parts)
    ]
    for load in loads:
        load.start()
    for load, store in zip(loads, stores):
        load.wait()
        store.start()
    for store in stores:
        store.wait()


def local(queries, outputs, out_grads, resp_keys, resp_values, lengths, prompt_keys, prompt_values):
    any_spec = pl.BlockSpec(memory_space=pl.ANY)
    pairs = GROUPS * PAIRS
    wide = (ROWS, pairs * WIDE)
    narrow = (ROWS, GROUPS * HEAD)
    block = (OWN, 2 * HEAD)
    half = (HALF, 2 * HEAD)
    shapes = [
        jax.ShapeDtypeStruct((1,) + wide, BF16),
        jax.ShapeDtypeStruct((1,) + narrow, BF16),
        jax.ShapeDtypeStruct((1,) + narrow, BF16),
        jax.ShapeDtypeStruct((OWN, GROUPS * HEAD), BF16),
        jax.ShapeDtypeStruct((OWN, GROUPS * HEAD), BF16),
    ]
    results = pl.pallas_call(
        kernel,
        name="grads",
        out_shape=shapes,
        in_specs=[any_spec] * 8,
        out_specs=[any_spec] * 5,
        scratch_shapes=[
            pltpu.VMEM(wide, BF16),
            pltpu.VMEM(wide, BF16),
            pltpu.VMEM(wide, BF16),
            pltpu.VMEM(narrow, BF16),
            pltpu.VMEM(narrow, BF16),
            pltpu.VMEM((GROUPS, PROMPT, 2 * HEAD), BF16),
            pltpu.VMEM((2, PROMPT, WIDE), F32),
            pltpu.VMEM((pairs, ROWS, WIDE), F32),
            pltpu.VMEM((pairs, ROWS, WIDE), F32),
            pltpu.VMEM((PAIRS, PROMPT, WIDE), BF16),
            pltpu.VMEM((pairs, ROWS, WIDE), BF16),
            pltpu.VMEM((pairs, KEYS, WIDE), BF16),
            pltpu.VMEM((pairs, 8, WIDE), F32),
            pltpu.VMEM((PROMPT, 2 * HEAD), F32),
            pltpu.VMEM((GROUPS,) + half, F32),
            pltpu.VMEM((GROUPS,) + half, BF16),
            pltpu.VMEM((GROUPS,) + half, BF16),
            pltpu.VMEM((GROUPS, 5) + block, BF16),
            pltpu.VMEM((GROUPS, 5) + block, BF16),
            pltpu.VMEM((GROUPS, 2) + block, BF16),
            pltpu.VMEM((GROUPS, 2) + block, BF16),
            pltpu.VMEM(wide, BF16),
            pltpu.VMEM(narrow, BF16),
            pltpu.VMEM(narrow, BF16),
            pltpu.VMEM((OWN, GROUPS * HEAD), BF16),
            pltpu.VMEM((OWN, GROUPS * HEAD), BF16),
            pltpu.SMEM((2 * CHIPS,), jnp.int32),
            pltpu.SemaphoreType.DMA((6,)),
            pltpu.SemaphoreType.DMA,
            pltpu.SemaphoreType.DMA((6,)),
            pltpu.SemaphoreType.DMA((GROUPS, 8)),
            pltpu.SemaphoreType.DMA((GROUPS, 8)),
            pltpu.SemaphoreType.DMA((GROUPS, 8)),
            pltpu.SemaphoreType.DMA((GROUPS, 8)),
        ],
        compiler_params=pltpu.CompilerParams(
            collective_id=0, has_side_effects=True, vmem_limit_bytes=56 * 2**20
        ),
        cost_estimate=pl.CostEstimate(flops=4700000000, bytes_accessed=5000000, transcendentals=3670016),
    )(queries, outputs, out_grads, resp_keys, resp_values, lengths, prompt_keys, prompt_values)
    return pl.pallas_call(
        finish,
        name="finish",
        out_shape=shapes,
        in_specs=[any_spec] * 5,
        out_specs=[any_spec] * 5,
        scratch_shapes=[pltpu.VMEM(shape.shape, shape.dtype) for shape in shapes]
        + [pltpu.SemaphoreType.DMA((8,))] * 2,
    )(*results)


def solution(mesh):
    rows = P(("dp", "seq"), None, None)
    prompt = P(("dp", "seq"), None)
    return jax.shard_map(
        local,
        mesh=mesh,
        in_specs=(rows, rows, rows, rows, rows, P("dp"), prompt, prompt),
        out_specs=(rows, rows, rows, prompt, prompt),
        check_vma=False,
    )
```
